32 devices in a mesh: gx: 8 (over z, y), gy: 4 (over x, core).
Axes of the slice: x: 2, y: 2, z: 4, core: 2. Of those that a mesh axis runs over, the one named last changes fastest.
Arguments:
- points: bfloat16 [256, 128, 512], P(('gx', 'gy')), may hold values from -6 to 6
- moved_to: int32 [2, 2, 256], P(None, None, ('gx', 'gy')), may hold values from 0 to 255, as said below
- gains: float32 [2, 2, 512], replicated, may hold values from 0.1 to 1.9
- w_qkv: bfloat16 [2, 512, 1536], replicated, may hold values from -4 to 4
- w_out: bfloat16 [2, 512, 512], replicated, may hold values from -0.25 to 0.25
- w_up: bfloat16 [2, 512, 2048], replicated, may hold values from -0.25 to 0.25
- w_down: bfloat16 [2, 2048, 512], replicated, may hold values from -0.125 to 0.125
Outputs:
- encoded: bfloat16 [256, 128, 512], P(('gx', 'gy'))
The draws below stay inside these ranges and needn't reach their ends.
Inputs may be any that keep to these rules, and one draw needn't show every extreme that they name: Each moved_to[l, s] is a permutation of the 256 positions. The owner of position p is p // 8, with owner index = gx index * 4 + gy index. Section 0 keeps every brick's gy index, section 1 its gx index. From one owner at most 2 bricks go to any one owner in section 0 and at most 2 in section 1; in every layer, section and group some owner sends exactly that many to one owner.
All inputs are finite; a program needn't handle non-finite values.
Results may differ from the reference program's by a relative error of at most 0.018.
Values may be sent and summed in bfloat16 or wider, within the bound.
No kernel may reach another device: no remote copies, remote signals or barrier semaphores. Data moves between devices by JAX's collectives and lax.ppermute only.
A program may use at most 128 MiB of HBM per device.

```python
import math
import jax
import jax.numpy as jnp
from jax import lax

D = 512
FF = 2048
HEAD_DIM = 16
BRICK = 128
PATCH = 512
LAYERS = 2
BR_DEV = 8
BRICKS = 256
N_GX = 8
N_GY = 4


def many_perms(key, count, length):
    return jax.vmap(lambda single: jax.random.permutation(single, length))(jax.random.split(key, count))


def section_targets(key, groups, peers, br):
    cap = max(2, -(-br // peers))
    split_keys = jax.random.split(key, 5)
    rotate = many_perms(split_keys[0], groups, peers)
    relabel = many_perms(split_keys[1], groups, peers)
    offsets = many_perms(split_keys[2], groups, peers)
    slots = jnp.arange(br)
    pick = jnp.where(slots < cap, 0, 1 + (slots - cap) % (peers - 1))
    offset_slot = offsets[:, pick]
    slot_of = many_perms(split_keys[3], groups * peers, br).reshape(groups, peers, br)
    place_of = many_perms(split_keys[4], groups * peers, br).reshape(groups, peers, br)
    offset_at = jnp.take_along_axis(jnp.broadcast_to(offset_slot[:, None, :], (groups, peers, br)), slot_of, axis=2)
    circle = (rotate[:, :, None] + offset_at) % peers
    target = jnp.take_along_axis(jnp.broadcast_to(relabel[:, None, :], (groups, peers, peers)), circle, axis=2)
    group_index = jnp.arange(groups)[:, None, None]
    position = place_of[group_index, target, slot_of]
    return (target, position)


def draw_moved_to(key, part):
    layers_out = []
    for layer in range(LAYERS):
        row_key = jax.random.fold_in(jax.random.fold_in(key, 101), layer)
        col_key = jax.random.fold_in(jax.random.fold_in(key, 202), layer)
        target, position = section_targets(row_key, N_GY, N_GX, BR_DEV)
        column = jnp.arange(N_GY)[:, None, None]
        first = ((target * N_GY + column) * BR_DEV + position).transpose(1, 0, 2).reshape(-1)
        target, position = section_targets(col_key, N_GX, N_GY, BR_DEV)
        row = jnp.arange(N_GX)[:, None, None]
        second = ((row * N_GY + target) * BR_DEV + position).reshape(-1)
        layers_out.append(jnp.stack([first, second]))
    return jnp.stack(layers_out).astype(jnp.int32)


def draw_w_qkv(key, part):
    base = jax.random.normal(key, (LAYERS, D, 3 * D), jnp.float32) * (1.0 / jnp.sqrt(jnp.float32(D)))
    return jnp.clip(base, -4.0, 4.0).astype(jnp.bfloat16)


def block_scale(rng, extent, cuts, low, top_value):
    factor_of = 1.0
    for dim, blocks in cuts:
        heights = jax.random.uniform(jax.random.fold_in(jax.random.fold_in(rng, 6), dim), (blocks,), jnp.float32, low / len(cuts), top_value / len(cuts))
        factor_of = factor_of * jnp.repeat(jnp.exp(heights), extent[dim] // blocks).reshape((-1,) + (1,) * (len(extent) - 1 - dim))
    return factor_of


def scatter_about(stream_key, extent, scale, reach, cuts=(), kind=jnp.bfloat16):
    level = block_scale(stream_key, extent, cuts, -0.22, 0.18) if cuts else 1.0
    array = jax.random.normal(stream_key, extent, jnp.float32) * scale * level
    return jnp.minimum(jnp.maximum(array, -reach), reach).astype(kind)


def setup_inputs(seed: int = 0) -> dict:
    key_list = jax.random.split(jax.random.key(seed), 8)
    return {
        "points": scatter_about(key_list[0], (BRICKS, BRICK, D), 1.0, 6.0, ((0, 32),)),
        "moved_to": draw_moved_to(jax.random.fold_in(key_list[7], 71), 0),
        "gains": jnp.clip(1.0 + 0.18 * jax.random.normal(key_list[2], (LAYERS, 2, D), jnp.float32), 0.1, 1.9),
        "w_qkv": draw_w_qkv(jax.random.fold_in(key_list[7], 71), 0),
        "w_out": scatter_about(key_list[4], (LAYERS, D, D), D ** -0.5, 0.25),
        "w_up": scatter_about(key_list[5], (LAYERS, D, FF), D ** -0.5, 0.25),
        "w_down": scatter_about(key_list[6], (LAYERS, FF, D), FF ** -0.5, 0.125),
    }


def normalize(values, gain):
    values = values.astype(jnp.float32)
    center = values - lax.optimization_barrier(jnp.mean(values, axis=1, keepdims=True))
    spread = lax.optimization_barrier(jnp.mean(center * center, axis=1, keepdims=True))
    return center * lax.rsqrt(spread + 1e-05) * gain

def attend_patch(patch):
    width = patch.shape[1] // 3
    count = patch.shape[0]
    heads = width // HEAD_DIM
    block = min(8, heads)
    scale = 1.0 / math.sqrt(HEAD_DIM)
    query = patch[:, :width].reshape(count, heads, HEAD_DIM).astype(jnp.float32)
    keys = patch[:, width:2 * width].reshape(count, heads, HEAD_DIM).astype(jnp.float32)
    values = patch[:, 2 * width:].reshape(count, heads, HEAD_DIM).astype(jnp.float32)
    pieces = []
    for first in range(0, heads, block):
        scores = jnp.einsum('qhd,khd->hqk', query[:, first:first + block], keys[:, first:first + block]) * scale
        peak = lax.optimization_barrier(jnp.max(scores, axis=2, keepdims=True))
        weights = jnp.exp(scores - peak)
        probs = (weights / lax.optimization_barrier(jnp.sum(weights, axis=2, keepdims=True))).astype(jnp.bfloat16)
        mixed = jnp.einsum('hqk,khd->qhd', probs.astype(jnp.float32), values[:, first:first + block])
        pieces.append(mixed.reshape(count, block * HEAD_DIM))
    return jnp.concatenate(pieces, axis=1).astype(jnp.bfloat16)

def encoder_layer(bricks, gain, w_qkv, w_out, w_up, w_down):
    shape = bricks.shape
    flat = bricks.reshape(-1, shape[2])
    normed = normalize(flat, gain[0]).astype(jnp.bfloat16)
    projected = jnp.dot(normed, w_qkv, preferred_element_type=jnp.float32).astype(jnp.bfloat16)
    attended = lax.map(attend_patch, projected.reshape(-1, PATCH, projected.shape[1])).reshape(flat.shape)
    mixed = (flat.astype(jnp.float32) + jnp.dot(attended, w_out, preferred_element_type=jnp.float32)).astype(jnp.bfloat16)
    inner = normalize(mixed, gain[1]).astype(jnp.bfloat16)
    hidden = jax.nn.gelu(jnp.dot(inner, w_up, preferred_element_type=jnp.float32), approximate=False).astype(jnp.bfloat16)
    result = mixed.astype(jnp.float32) + jnp.dot(hidden, w_down, preferred_element_type=jnp.float32)
    return result.astype(jnp.bfloat16).reshape(shape)

def reference(points, moved_to, gains, w_qkv, w_out, w_up, w_down):
    bricks = points
    for layer in range(LAYERS):
        for section in range(2):
            bricks = jnp.zeros_like(bricks).at[moved_to[layer, section]].set(bricks)
        bricks = encoder_layer(bricks, gains[layer], w_qkv[layer], w_out[layer], w_up[layer], w_down[layer])
    return bricks
```

```python
import functools
import math

import jax
import jax.numpy as jnp
from jax import lax
from jax.experimental import pallas as pl
from jax.experimental.pallas import tpu as pltpu
from jax.sharding import PartitionSpec as P

HEAD_DIM = 16
PATCH = 512
LAYERS = 2
LANES = 128
CHUNKS = 1
UNROLL = 4
FF_BLOCK = 512
BF16 = jnp.bfloat16
F32 = jnp.float32


def normalize(values, gain):
    center = values - jnp.mean(values, axis=1, keepdims=True)
    spread = jnp.mean(center * center, axis=1, keepdims=True)
    return center * lax.rsqrt(spread + 1e-05) * gain


def matmul(left, right, dims=((1,), (0,))):
    return lax.dot_general(left, right, (dims, ((), ())), preferred_element_type=F32)


def layer_kernel(layer, n_in, n_out, order_ref, slot_ref, *refs):
    inputs, refs = refs[:n_in], refs[n_in:]
    gain_ref, *hbm_weights = refs[:5]
    outputs, refs = refs[5 : 5 + n_out], refs[5 + n_out :]
    x_ref, y_ref, q_ref, k_ref, vt_ref, ot_ref, *rest = refs
    weights, (in_sems, out_sems, w_sems) = rest[:4], rest[4:]
    wqkv_ref, wout_ref, wup_ref, wdown_ref = weights
    count, rows, width = x_ref.shape
    heads = width // HEAD_DIM
    per_patch = PATCH // rows
    patch = pl.program_id(0)

    def load(brick, piece):
        span = width // n_in
        return pltpu.make_async_copy(
            inputs[piece].at[order_ref[brick]],
            x_ref.at[brick, :, pl.ds(piece * span, span)],
            in_sems.at[brick, piece],
        )

    def store(brick, piece):
        span = width // n_out
        return pltpu.make_async_copy(
            y_ref.at[brick, :, pl.ds(piece * span, span)],
            outputs[piece].at[slot_ref[brick]],
            out_sems.at[brick, piece],
        )

    def fetch(which):
        return pltpu.make_async_copy(
            hbm_weights[which].at[layer], weights[which], w_sems.at[which]
        )

    def arrive(which):
        @pl.when(patch == 0)
        def _():
            fetch(which).wait()

    @pl.when(patch == 0)
    def _():
        for brick in range(count):
            for piece in range(n_in):
                load(brick, piece).start()
            if brick + 1 == per_patch:
                for which in range(4):
                    fetch(which).start()
        vt_ref[:, HEAD_DIM:, :] = jnp.ones((heads, HEAD_DIM, PATCH), BF16)

    first = patch * per_patch
    for brick in range(per_patch):
        for piece in range(n_in):
            load(first + brick, piece).wait()

    x = x_ref[pl.ds(first, per_patch)].reshape(PATCH, width)
    normed = normalize(x.astype(F32), gain_ref[layer, 0:1, :]).astype(BF16)
    arrive(0)
    scale = math.log2(math.e) / math.sqrt(HEAD_DIM)
    q_ref[...] = (matmul(normed, wqkv_ref[:, :width]) * scale).astype(BF16)
    k_ref[...] = matmul(normed, wqkv_ref[:, width : 2 * width]).astype(BF16)
    values = matmul(normed, wqkv_ref[:, 2 * width :]).T.astype(BF16)
    vt_ref[:, :HEAD_DIM, :] = values.reshape(heads, HEAD_DIM, PATCH)

    lane_head = lax.broadcasted_iota(jnp.int32, (PATCH, LANES), 1) // HEAD_DIM
    per_tile = LANES // HEAD_DIM

    @pl.loop(0, heads // UNROLL)
    def _(group):
        for step in range(UNROLL):
            head = group * UNROLL + step
            column = pl.multiple_of(head // per_tile * LANES, LANES)
            queries = q_ref[:, pl.ds(column, LANES)]
            queries = jnp.where(lane_head == head % per_tile, queries, jnp.zeros_like(queries))
            scores = matmul(k_ref[:, pl.ds(column, LANES)], queries, ((1,), (1,)))
            scores = scores - jnp.max(scores, axis=0, keepdims=True)
            probs = jnp.exp2(scores).astype(BF16)
            mixed = matmul(vt_ref[head], probs)
            spot = pl.ds(pl.multiple_of(head * HEAD_DIM, HEAD_DIM), HEAD_DIM)
            share = 1.0 / mixed[HEAD_DIM : HEAD_DIM + 1]
            ot_ref[spot, :] = (mixed[:HEAD_DIM] * share).astype(BF16)

    arrive(1)
    mixed = (x.astype(F32) + matmul(ot_ref[...], wout_ref[...], ((0,), (0,)))).astype(BF16)
    inner = normalize(mixed.astype(F32), gain_ref[layer, 1:2, :]).astype(BF16)
    total = mixed.astype(F32)
    arrive(2)
    arrive(3)
    for start in range(0, wup_ref.shape[1], FF_BLOCK):
        up = matmul(inner, wup_ref[:, start : start + FF_BLOCK])
        half = up * 0.5
        hidden = (half + half * lax.erf(up * math.sqrt(0.5))).astype(BF16)
        total = total + matmul(hidden, wdown_ref[start : start + FF_BLOCK, :])
    y_ref[pl.ds(first, per_patch)] = total.astype(BF16).reshape(per_patch, rows, width)

    for brick in range(per_patch):
        for piece in range(n_out):
            store(first + brick, piece).start()

    @pl.when(patch == pl.num_programs(0) - 1)
    def _():
        for brick in range(count):
            for piece in range(n_out):
                store(brick, piece).wait()


def encoder_layer(layer, pieces, order, slots, n_slots, n_out, gains, weights):
    n_in = len(pieces)
    rows, width = pieces[0].shape[1], pieces[0].shape[2] * n_in
    count = order.shape[0]
    heads = width // HEAD_DIM
    hbm = pl.BlockSpec(memory_space=pl.ANY)
    smem = pl.BlockSpec(memory_space=pltpu.SMEM)
    vmem = pl.BlockSpec(memory_space=pltpu.VMEM)
    return pl.pallas_call(
        functools.partial(layer_kernel, layer, n_in, n_out),
        grid=(count * rows // PATCH,),
        in_specs=[smem, smem] + [hbm] * n_in + [vmem] + [hbm] * 4,
        out_specs=[hbm] * n_out,
        out_shape=[jax.ShapeDtypeStruct((n_slots, rows, width // n_out), BF16)] * n_out,
        scratch_shapes=[
            pltpu.VMEM((count, rows, width), BF16),
            pltpu.VMEM((count, rows, width), BF16),
            pltpu.VMEM((PATCH, width), BF16),
            pltpu.VMEM((PATCH, width), BF16),
            pltpu.VMEM((heads, 2 * HEAD_DIM, PATCH), BF16),
            pltpu.VMEM((width, PATCH), BF16),
        ]
        + [pltpu.VMEM(weight.shape[1:], BF16) for weight in weights]
        + [
            pltpu.SemaphoreType.DMA((count, n_in)),
            pltpu.SemaphoreType.DMA((count, n_out)),
            pltpu.SemaphoreType.DMA((4,)),
        ],
        compiler_params=pltpu.CompilerParams(vmem_limit_bytes=48 * 2**20),
    )(order, slots, *pieces, gains, *weights)


def ranks(targets):
    count = targets.shape[-1]
    same = targets[..., :, None] == targets[..., None, :]
    earlier = jnp.arange(count)[None, :] < jnp.arange(count)[:, None]
    return jnp.sum((same & earlier).astype(jnp.int32), axis=-1)


def lookup(keys, wanted, found):
    hit = keys[..., None, :] == wanted[..., :, None]
    return jnp.sum(jnp.where(hit, found[..., None, :], 0), axis=-1)


def per_device(points, moved_to, gains, *weights):
    count = points.shape[0]
    peers = {"gx": lax.axis_size("gx"), "gy": lax.axis_size("gy")}
    columns = peers["gy"]
    me = lax.axis_index("gx") * columns + lax.axis_index("gy")
    room = [max(2, -(-count // peers["gx"])), max(2, -(-count // peers["gy"]))]

    def target(moved):
        owner = moved // count
        return jnp.stack([owner[:, 0] // columns, owner[:, 1] % columns], axis=1)

    size = jnp.array(room)[None, :, None]
    local_target = target(moved_to)
    local_slot = local_target * size + ranks(local_target)
    width = points.shape[2] // CHUNKS

    swap = functools.partial(lax.all_to_all, split_axis=0, concat_axis=0, tiled=True)
    devices = peers["gx"] * peers["gy"]
    total = devices * count
    everyone = swap(jnp.broadcast_to(moved_to[None], (devices,) + moved_to.shape), ("gx", "gy"))
    everyone = everyone.transpose(1, 2, 0, 3).reshape(LAYERS, 2, total)
    owners = everyone.reshape(LAYERS, 2, total // count, count)
    whole_target = target(everyone)
    rank = ranks(whole_target.reshape(owners.shape)).reshape(everyone.shape)
    source = jnp.arange(total) // count
    source = jnp.stack([source // columns, source % columns])[None]
    landing = source * size + rank
    mine = me * count + jnp.arange(count)
    mine = jnp.broadcast_to(mine, (LAYERS, 2, count))
    arrival = lookup(everyone, mine, landing)
    second = jnp.arange(peers["gy"] * room[1])
    resend = lookup(
        local_slot[:, 1], jnp.broadcast_to(second, (LAYERS,) + second.shape), arrival[:, 0]
    )

    slots = jnp.arange(peers["gx"] * room[0])
    source = lookup(local_slot[0, 0], slots, jnp.arange(count))
    pieces = [
        jnp.take(points[:, :, i * width : (i + 1) * width], source, axis=0) for i in range(CHUNKS)
    ]
    for layer in range(LAYERS):
        pieces = [swap(piece, "gx") for piece in pieces]
        pieces = [jnp.take(piece, resend[layer], axis=0) for piece in pieces]
        pieces = [swap(piece, "gy") for piece in pieces]
        last = layer + 1 == LAYERS
        pieces = encoder_layer(
            layer,
            pieces,
            arrival[layer, 1],
            jnp.arange(count) if last else local_slot[layer + 1, 0],
            count if last else slots.shape[0],
            1 if last else CHUNKS,
            gains,
            weights,
        )
    return pieces[0]


def solution(mesh):
    placed = (P(("gx", "gy"), None, None), P(None, None, ("gx", "gy")), P(), P(), P(), P(), P())
    return jax.shard_map(
        per_device,
        mesh=mesh,
        in_specs=placed,
        out_specs=P(("gx", "gy"), None, None),
        check_vma=False,
    )
```

```python
import functools
import math

import jax
import jax.numpy as jnp
from jax import lax
from jax.experimental import pallas as pl
from jax.experimental.pallas import tpu as pltpu
from jax.sharding import PartitionSpec as P

HEAD_DIM = 16
PATCH = 512
LAYERS = 2
LANES = 128
WAYS = 4
FF_BLOCK = 512
BF16 = jnp.bfloat16
F32 = jnp.float32
HBM = pl.BlockSpec(memory_space=pltpu.HBM)
SMEM = pl.BlockSpec(memory_space=pltpu.SMEM)
VMEM = pl.BlockSpec(memory_space=pltpu.VMEM)


def normalize(values, gain):
    center = values - jnp.mean(values, axis=1, keepdims=True)
    spread = jnp.mean(center * center, axis=1, keepdims=True)
    return center * lax.rsqrt(spread + 1e-05) * gain


def matmul(left, right, dims=((1,), (0,))):
    return lax.dot_general(left, right, (dims, ((), ())), preferred_element_type=F32)


def start(copy):
    copy.start()


def wait(copy):
    copy.wait()


def send_bricks(action, patch, bricks, tables, payload, spare, hops, sems):
    pick_ref, spare_ref = tables
    size, rows, width = bricks.shape
    peers = len(payload)

    def here(brick):
        return (brick >= patch * size) & (brick < (patch + 1) * size)

    for shift in range(peers):
        brick = pick_ref[shift]

        @pl.when(here(brick))
        def _():
            source = bricks.at[brick - patch * size]
            action(
                pltpu.make_async_copy(source, payload[shift].at[pl.ds(0, rows)], sems.at[0, shift])
            )

    for place in range(spare.shape[0]):
        brick = spare_ref[place]

        @pl.when(here(brick))
        def _():
            source = bricks.at[brick - patch * size]
            action(pltpu.make_async_copy(source, spare.at[place], sems.at[1, place]))

    brick = spare_ref[0]

    @pl.when(here(brick))
    def _():
        source = bricks.at[brick - patch * size]
        tall = rows // len(hops)
        for way in range(len(hops)):
            window = pl.ds(way * tall, tall)
            action(pltpu.make_async_copy(source.at[window], hops[way], sems.at[2, way]))


def pack_kernel(pick_ref, spare_ref, points, *refs):
    peers = pick_ref.shape[0]
    payload, spare, hops, sems = refs[:peers], refs[peers], refs[peers + 1 : -1], refs[-1]
    for action in (start, wait):
        send_bricks(action, 0, points, (pick_ref, spare_ref), payload, spare, hops, sems)


def relay_kernel(ways, relay_ref, *refs):
    peers = relay_ref.shape[0]
    hops, payload = refs[:ways], refs[ways + peers : ways + 2 * peers]
    staged, in_sems, out_sems = refs[ways + 2 * peers :]
    _, tall, _ = staged.shape
    rows = payload[0].shape[0] - tall
    for action in (start, wait):
        for way in range(ways):
            action(pltpu.make_async_copy(hops[way], staged.at[way], in_sems.at[way]))
    for action in (start, wait):
        for shift in range(peers):

            @pl.when(relay_ref[shift] >= 0)
            def _():
                action(
                    pltpu.make_async_copy(
                        staged.at[relay_ref[shift]],
                        payload[shift].at[pl.ds(rows, tall)],
                        out_sems.at[shift],
                    )
                )


def turn_kernel(peers, kind_ref, source_ref, *refs):
    arrived, second, refs = refs[:peers], refs[peers], refs[peers + 1 :]
    outs, (staged, extra, in_sems, out_sems) = refs[:-4], refs[-4:]
    room, rows, width = outs[0].shape
    tall = rows // WAYS
    stride = peers // WAYS
    for action in (start, wait):
        for shift in range(peers):
            action(pltpu.make_async_copy(arrived[shift], staged.at[shift], in_sems.at[shift]))
    for slot in range(kind_ref.shape[0]):
        out, sem = outs[slot // room].at[slot % room], out_sems.at[slot]

        @pl.when(kind_ref[slot] == 0)
        def _():
            pltpu.make_async_copy(
                staged.at[source_ref[slot], pl.ds(0, rows)], out, sem
            ).start()

        @pl.when(kind_ref[slot] == 1)
        def _():
            for way in range(WAYS):
                shift = (source_ref[slot] - way * stride + peers) % peers
                pltpu.make_async_copy(
                    staged.at[shift, pl.ds(rows, tall)], out.at[pl.ds(way * tall, tall)], sem
                ).start()

        @pl.when(kind_ref[slot] == 2)
        def _():
            copy = pltpu.make_async_copy(
                second.at[source_ref[slot]], extra.at[slot], in_sems.at[peers + slot]
            )
            copy.start()
            copy.wait()
            pltpu.make_async_copy(extra.at[slot], out, sem).start()

    for slot in range(kind_ref.shape[0]):
        out = outs[slot // room].at[slot % room]
        pltpu.make_async_copy(extra.at[slot], out, out_sems.at[slot]).wait()


def attend(q_ref, k_ref, v_ref, mixed_ref):
    tiles, count, _ = v_ref.shape
    head_of = lax.broadcasted_iota(jnp.int32, (count, LANES), 1) // HEAD_DIM
    per_tile = LANES // HEAD_DIM

    def weigh(queries, keys, values, head, shifted):
        chosen = jnp.where(head_of == head, queries, jnp.zeros_like(queries))
        scores = matmul(chosen, keys, ((1,), (1,)))
        if shifted:
            scores = scores - jnp.max(scores, axis=1, keepdims=True)
        return matmul(jnp.exp2(scores).astype(BF16), values)

    low = jnp.full((count, LANES), 1.0, F32)
    high = jnp.full((count, LANES), 1.0, F32)
    for tile in range(tiles):
        column = pl.ds(tile * LANES, LANES)
        queries, keys, values = q_ref[:, column], k_ref[:, column], v_ref[tile]
        above = jnp.zeros((count, LANES), F32)
        below = jnp.ones((count, LANES), F32)
        for head in range(per_tile):
            sums = weigh(queries, keys, values, head, False)
            above = jnp.where(head_of == head, sums[:, :LANES], above)
            below = jnp.where(head_of == head, sums[:, LANES:], below)
        mixed_ref[:, column] = (above / below).astype(BF16)
        low = jnp.minimum(low, below)
        high = jnp.maximum(high, below)
    safe = (jnp.min(low) > 2.0**-60) & (jnp.max(high) < 2.0**100)

    @pl.when(jnp.logical_not(safe))
    def _():
        @pl.loop(0, tiles)
        def _(tile):
            column = pl.ds(pl.multiple_of(tile * LANES, LANES), LANES)

            @pl.loop(0, per_tile)
            def _(head):
                sums = weigh(q_ref[:, column], k_ref[:, column], v_ref[tile], head, True)
                mixed = (sums[:, :LANES] / sums[:, LANES:]).astype(BF16)
                mixed_ref[:, column] = jnp.where(head_of == head, mixed, mixed_ref[:, column])


def layer_kernel(layer, columns, peers, order_ref, *refs):
    tables, refs = refs[:2], refs[2:]
    arrived, gain_ref = refs[:columns], refs[columns]
    hbm_weights, refs = refs[columns + 1 : columns + 5], refs[columns + 5 :]
    n_out = peers + 1 + WAYS if peers else 1
    outputs, refs = refs[:n_out], refs[n_out:]
    x_ref, y_ref, q_ref, k_ref, v_ref, mixed_ref = refs[:6]
    weights, (in_sems, out_sems, w_sems) = refs[6:10], refs[10:]
    wqkv_ref, wout_ref, wup_ref, wdown_ref = weights
    patches, per_patch, rows, width = y_ref.shape
    room = arrived[0].shape[0]
    turn = pl.program_id(0)

    def load(piece):
        return pltpu.make_async_copy(
            arrived[piece], x_ref.at[pl.ds(piece * room, room)], in_sems.at[piece]
        )

    def store(action, step):
        if peers:
            send_bricks(
                action, step, y_ref.at[step], tables, outputs[:peers], outputs[peers],
                outputs[peers + 1 :], out_sems,
            )
        else:
            spot = pl.ds(step * per_patch, per_patch)
            action(pltpu.make_async_copy(y_ref.at[step], outputs[0].at[spot], out_sems.at[0, step]))

    def fetch(which):
        return pltpu.make_async_copy(
            hbm_weights[which].at[layer], weights[which], w_sems.at[which]
        )

    def arrive(which):
        @pl.when(turn == 0)
        def _():
            fetch(which).wait()

    @pl.when(turn == 0)
    def _():
        for piece in range(columns):
            load(piece).start()
        for which in range(4):
            fetch(which).start()
        v_ref[:, :, LANES:] = jnp.ones(v_ref.shape[:2] + (LANES,), BF16)
        for piece in range(columns):
            load(piece).wait()

    first = turn * per_patch
    x = jnp.concatenate([x_ref[order_ref[first + brick]] for brick in range(per_patch)], axis=0)
    normed = normalize(x.astype(F32), gain_ref[layer, 0:1, :]).astype(BF16)
    arrive(0)
    scale = math.log2(math.e) / math.sqrt(HEAD_DIM)
    q_ref[...] = (matmul(normed, wqkv_ref[:, :width]) * scale).astype(BF16)
    k_ref[...] = matmul(normed, wqkv_ref[:, width : 2 * width]).astype(BF16)
    values = matmul(normed, wqkv_ref[:, 2 * width :]).astype(BF16)
    for tile in range(width // LANES):
        v_ref[tile, :, :LANES] = values[:, tile * LANES : (tile + 1) * LANES]

    attend(q_ref, k_ref, v_ref, mixed_ref)

    arrive(1)
    mixed = (x.astype(F32) + matmul(mixed_ref[...], wout_ref[...])).astype(BF16)
    inner = normalize(mixed.astype(F32), gain_ref[layer, 1:2, :]).astype(BF16)
    total = mixed.astype(F32)
    arrive(2)
    arrive(3)
    for begin in range(0, wup_ref.shape[1], FF_BLOCK):
        up = matmul(inner, wup_ref[:, begin : begin + FF_BLOCK])
        half = up * 0.5
        hidden = (half + half * lax.erf(up * math.sqrt(0.5))).astype(BF16)
        total = total + matmul(hidden, wdown_ref[begin : begin + FF_BLOCK, :])
    y_ref[turn] = total.astype(BF16).reshape(per_patch, rows, width)
    store(start, turn)

    @pl.when(turn == patches - 1)
    def _():
        for step in range(patches):
            store(wait, step)


def send_shapes(count, rows, width, peers):
    tall = rows // WAYS
    shapes = [jax.ShapeDtypeStruct((rows + tall, width), BF16)] * peers
    shapes += [jax.ShapeDtypeStruct((max(1, count // 2), rows, width), BF16)]
    return shapes + [jax.ShapeDtypeStruct((tall, width), BF16)] * WAYS


def pack(points, tables):
    count, rows, width = points.shape
    peers = tables[0].shape[0]
    shapes = send_shapes(count, rows, width, peers)
    return pl.pallas_call(
        pack_kernel,
        in_specs=[SMEM] * 2 + [VMEM],
        out_specs=[HBM] * len(shapes),
        out_shape=shapes,
        scratch_shapes=[pltpu.SemaphoreType.DMA((3, max(peers, count)))],
    )(*tables, points)


def relay(picks, hops, payload):
    peers = len(payload)
    return pl.pallas_call(
        functools.partial(relay_kernel, len(hops)),
        in_specs=[SMEM] + [HBM] * (len(hops) + peers),
        out_specs=[HBM] * peers,
        out_shape=[jax.ShapeDtypeStruct(slot.shape, BF16) for slot in payload],
        input_output_aliases={1 + len(hops) + i: i for i in range(peers)},
        scratch_shapes=[
            pltpu.VMEM((len(hops),) + hops[0].shape, BF16),
            pltpu.SemaphoreType.DMA((len(hops),)),
            pltpu.SemaphoreType.DMA((peers,)),
        ],
    )(picks, *hops, *payload)


def turn_bricks(kind, source, arrived, second, columns):
    peers, slots = len(arrived), kind.shape[0]
    brick = second.shape[1:]
    return pl.pallas_call(
        functools.partial(turn_kernel, peers),
        in_specs=[SMEM] * 2 + [HBM] * (peers + 1),
        out_specs=[HBM] * columns,
        out_shape=[jax.ShapeDtypeStruct((slots // columns,) + brick, BF16)] * columns,
        scratch_shapes=[
            pltpu.VMEM((peers,) + arrived[0].shape, BF16),
            pltpu.VMEM((slots,) + brick, BF16),
            pltpu.SemaphoreType.DMA((peers + slots,)),
            pltpu.SemaphoreType.DMA((slots,)),
        ],
        compiler_params=pltpu.CompilerParams(vmem_limit_bytes=32 * 2**20),
    )(kind, source, *arrived, second)


def encoder_layer(layer, arrived, order, tables, gains, weights, last=False):
    columns = len(arrived)
    room, rows, width = arrived[0].shape
    count = order.shape[0]
    patches = count * rows // PATCH
    per_patch = PATCH // rows
    peers = 0 if last else tables[0].shape[0]
    if last:
        shapes = [jax.ShapeDtypeStruct((count, rows, width), BF16)]
    else:
        shapes = send_shapes(count, rows, width, peers)
    tokens = patches * PATCH
    dense = sum(2 * tokens * weight.shape[1] * weight.shape[2] for weight in weights)
    heads = width // HEAD_DIM
    return pl.pallas_call(
        functools.partial(layer_kernel, layer, columns, peers),
        grid=(patches,),
        in_specs=[SMEM] * 3 + [HBM] * columns + [VMEM] + [HBM] * 4,
        out_specs=[HBM] * len(shapes),
        out_shape=shapes,
        scratch_shapes=[
            pltpu.VMEM((columns * room, rows, width), BF16),
            pltpu.VMEM((patches, per_patch, rows, width), BF16),
            pltpu.VMEM((PATCH, width), BF16),
            pltpu.VMEM((PATCH, width), BF16),
            pltpu.VMEM((width // LANES, PATCH, 2 * LANES), BF16),
            pltpu.VMEM((PATCH, width), BF16),
        ]
        + [pltpu.VMEM(weight.shape[1:], BF16) for weight in weights]
        + [
            pltpu.SemaphoreType.DMA((columns,)),
            pltpu.SemaphoreType.DMA((3, max(count, peers))),
            pltpu.SemaphoreType.DMA((4,)),
        ],
        compiler_params=pltpu.CompilerParams(vmem_limit_bytes=48 * 2**20),
        cost_estimate=pl.CostEstimate(
            flops=dense + 8 * tokens * PATCH * heads * LANES,
            bytes_accessed=4 * tokens * width + sum(2 * w.shape[1] * w.shape[2] for w in weights),
            transcendentals=tokens * PATCH * heads,
        ),
    )(order, *tables, *arrived, gains, *weights)


def ranks(targets):
    count = targets.shape[-1]
    same = targets[..., :, None] == targets[..., None, :]
    earlier = jnp.arange(count)[None, :] < jnp.arange(count)[:, None]
    return jnp.sum((same & earlier).astype(jnp.int32), axis=-1)


def lookup(keys, wanted, found):
    hit = keys[..., None, :] == wanted[..., :, None]
    return jnp.sum(jnp.where(hit, found[..., None, :], 0), axis=-1)


def most(keys, values, chosen):
    hit = (keys[..., None, :] == values[:, None]) & chosen[..., None, :]
    return jnp.max(jnp.sum(hit.astype(jnp.int32), axis=-1))


def shifted(arrays, axis):
    size = lax.axis_size(axis)
    step = size // len(arrays)
    return [arrays[0]] + [
        lax.ppermute(arrays[d], axis, [(i, (i + d * step) % size) for i in range(size)])
        for d in range(1, len(arrays))
    ]


def per_device(points, moved_to, gains, *weights):
    count, rows, width = points.shape
    peers, columns = lax.axis_size("gx"), lax.axis_size("gy")
    row, column = lax.axis_index("gx"), lax.axis_index("gy")
    me = row * columns + column
    devices = peers * columns
    total = devices * count
    room = max(2, -(-count // columns))
    swap = functools.partial(lax.all_to_all, split_axis=0, concat_axis=0, tiled=True)
    bricks = jnp.arange(count)
    shifts = jnp.arange(peers)
    stride = peers // WAYS

    ahead = (moved_to[:, 0] // count // columns - row) % peers
    late = ranks(ahead) > 0
    pick = lookup(jnp.where(late, -1, ahead), shifts, bricks + 1) - 1
    place = jnp.where(late, jnp.cumsum(late.astype(jnp.int32), axis=1) - 1, -1)
    spare = lookup(place, jnp.arange(max(1, count // 2)), bricks + 1) - 1
    across = (moved_to[:, 1] // count - column) % columns
    across_slot = across * room + ranks(across)
    tables = [(pick[layer], spare[layer]) for layer in range(LAYERS)]

    everyone = swap(jnp.broadcast_to(moved_to[None], (devices,) + moved_to.shape), ("gx", "gy"))
    targets = everyone[:, :, 0] // count // columns
    behind = ranks(targets) > 0
    opening = behind & (jnp.cumsum(behind.astype(jnp.int32), axis=-1) == 1)
    relayed = jnp.sum(jnp.where(opening, targets + 1, 0), axis=-1) - 1
    flat = lambda values: values.transpose(1, 0, 2).reshape(LAYERS, total)
    first, second = flat(everyone[:, :, 0]), flat(everyone[:, :, 1])
    behind = flat(behind)
    owner = jnp.arange(total) // count

    def crowded(layer):
        out = jnp.sum(behind[layer].reshape(devices, count).astype(jnp.int32), axis=1)
        return (jnp.max(out) > 1) | (
            most(first[layer] // count, jnp.arange(devices), behind[layer]) > 1
        )

    across_rank = flat(ranks(everyone[:, :, 1] // count % columns))
    mine = me * count + bricks
    slots = jnp.arange(columns * room)
    every = jnp.arange(devices)
    in_column = every % columns == column
    plans = []
    for layer in range(LAYERS):
        extra = crowded(layer)
        goal = jnp.where(in_column & (relayed[:, layer] >= 0), (relayed[:, layer] - row) % peers, -1)
        behind_me = (row - every // columns) % peers
        hit = (goal[None, :] == shifts[:, None]) & (behind_me % stride == 0)[None, :]
        relays = jnp.max(jnp.where(hit, behind_me[None, :] // stride, -1), axis=1)
        origin = lookup(first[layer], mine, (row - owner // columns) % peers)
        kind = lookup(first[layer], mine, jnp.where(behind[layer], jnp.where(extra, 2, 1), 0))
        slot_kind = lookup(across_slot[layer], slots, kind)
        slot_origin = lookup(across_slot[layer], slots, origin)
        order = lookup(
            second[layer], mine, (column - owner % columns) % columns * room + across_rank[layer]
        )
        plans.append((extra, relays, slot_kind, slot_origin, order))

    made = pack(points, tables[0])
    for layer in range(LAYERS):
        extra, relays, slot_kind, slot_origin, order = plans[layer]
        payload, spares, hops = made[:peers], made[peers], made[peers + 1 :]
        hops = shifted(hops, "gx")
        payload = relay(relays, hops, payload)
        arrived = shifted(payload, "gx")

        def send_second(spares, layer=layer):
            target = (ahead[layer] + row) % peers
            ready = lookup(jnp.where(late[layer], target, -1), shifts, place[layer])
            landed = swap(jnp.take(spares, ready, axis=0), "gx")
            return jnp.take(landed, (row - shifts) % peers, axis=0)

        def send_nothing(spares):
            return jnp.zeros((peers, rows, width), BF16)

        spares, arrived[1] = lax.optimization_barrier((spares, arrived[1]))
        seconds = lax.cond(extra, send_second, send_nothing, spares)
        arrived = turn_bricks(slot_kind, slot_origin, arrived, seconds, columns)
        arrived = shifted(arrived, "gy")
        last = layer + 1 == LAYERS
        made = encoder_layer(
            layer, arrived, order, tables[(layer + 1) % LAYERS], gains, weights, last
        )
    return made[0]


def solution(mesh):
    placed = (P(("gx", "gy"), None, None), P(None, None, ("gx", "gy")), P(), P(), P(), P(), P())
    return jax.shard_map(
        per_device,
        mesh=mesh,
        in_specs=placed,
        out_specs=P(("gx", "gy"), None, None),
        check_vma=False,
    )
```

```python
import functools
import math

import jax
import jax.numpy as jnp
from jax import lax
from jax.experimental import pallas as pl
from jax.experimental.pallas import tpu as pltpu
from jax.sharding import PartitionSpec as P

HEAD_DIM = 16
PATCH = 512
LAYERS = 2
LANES = 128
WAYS = 4
TAG_ROWS = 16
FF_BLOCK = 512
BF16 = jnp.bfloat16
F32 = jnp.float32
HBM = pl.BlockSpec(memory_space=pl.ANY)
SMEM = pl.BlockSpec(memory_space=pltpu.SMEM)
VMEM = pl.BlockSpec(memory_space=pltpu.VMEM)


def normalize(values, gain):
    center = values - jnp.mean(values, axis=1, keepdims=True)
    spread = jnp.mean(center * center, axis=1, keepdims=True)
    return center * lax.rsqrt(spread + 1e-05) * gain


def matmul(left, right, dims=((1,), (0,))):
    return lax.dot_general(left, right, (dims, ((), ())), preferred_element_type=F32)


def start(copy):
    copy.start()


def wait(copy):
    copy.wait()


def send_bricks(action, patch, bricks, tables, payload, spare, hops, sems, tag=None):
    pick_ref, spare_ref = tables
    size, rows, width = bricks.shape
    peers = len(payload)

    def here(brick):
        return (brick >= patch * size) & (brick < (patch + 1) * size)

    for shift in range(peers):
        brick = pick_ref[shift]

        @pl.when(here(brick))
        def _():
            source = bricks.at[brick - patch * size]
            action(
                pltpu.make_async_copy(source, payload[shift].at[pl.ds(0, rows)], sems.at[0, shift])
            )

    for place in range(spare.shape[0]):
        brick = spare_ref[place]

        @pl.when(here(brick))
        def _():
            source = bricks.at[brick - patch * size]
            action(pltpu.make_async_copy(source, spare.at[place], sems.at[1, place]))

    brick = spare_ref[0]

    @pl.when(here(brick))
    def _():
        source = bricks.at[brick - patch * size]
        tall = rows // len(hops)
        for way in range(len(hops)):
            window = pl.ds(way * tall, tall)
            target = hops[way].at[pl.ds(0, tall)]
            action(pltpu.make_async_copy(source.at[window], target, sems.at[2, way]))

    if tag is not None:
        tall = hops[0].shape[0] - TAG_ROWS
        for way in range(len(hops)):
            target = hops[way].at[pl.ds(tall, TAG_ROWS), pl.ds(0, LANES)]
            action(pltpu.make_async_copy(tag, target, sems.at[3, way]))


def pack_kernel(pick_ref, spare_ref, tag, points, *refs):
    peers = pick_ref.shape[0]
    payload, spare, hops, sems = refs[:peers], refs[peers], refs[peers + 1 : -1], refs[-1]
    for action in (start, wait):
        send_bricks(action, 0, points, (pick_ref, spare_ref), payload, spare, hops, sems, tag)


def relay_kernel(ways, tagged, goal_ref, *refs):
    peers = (len(refs) - 4 - ways) // 2
    hops, payload = refs[:ways], refs[ways + peers : ways + 2 * peers]
    staged, tags, in_sems, out_sems = refs[ways + 2 * peers :]
    _, tall, _ = staged.shape
    rows = payload[0].shape[0] - tall
    for action in (start, wait):
        for way in range(ways):
            source = hops[way].at[pl.ds(0, tall)]
            action(pltpu.make_async_copy(source, staged.at[way], in_sems.at[0, way]))
            if tagged:
                source = hops[way].at[pl.ds(tall, TAG_ROWS), pl.ds(0, LANES)]
                action(pltpu.make_async_copy(source, tags.at[way], in_sems.at[1, way]))
    goals = []
    for way in range(ways):
        if tagged:
            tag = jnp.max(tags[way].astype(F32)).astype(jnp.int32)
            ahead = (tag - 1 - way * (peers // ways) + peers) % peers
            goals.append(jnp.where(tag > 0, ahead, -1))
        else:
            goals.append(goal_ref[way])
    for action in (start, wait):
        for way in range(ways):
            for shift in range(peers):

                @pl.when(goals[way] == shift)
                def _():
                    target = payload[shift].at[pl.ds(rows, tall)]
                    action(pltpu.make_async_copy(staged.at[way], target, out_sems.at[way]))


def turn_kernel(peers, kind_ref, source_ref, *refs):
    arrived, second, refs = refs[:peers], refs[peers], refs[peers + 1 :]
    outs, (staged, extra, in_sems, out_sems) = refs[:-4], refs[-4:]
    room, rows, width = outs[0].shape
    tall = rows // WAYS
    stride = peers // WAYS
    for action in (start, wait):
        for shift in range(peers):
            action(pltpu.make_async_copy(arrived[shift], staged.at[shift], in_sems.at[shift]))
    for slot in range(kind_ref.shape[0]):
        out, sem = outs[slot // room].at[slot % room], out_sems.at[slot]

        @pl.when(kind_ref[slot] == 0)
        def _():
            pltpu.make_async_copy(
                staged.at[source_ref[slot], pl.ds(0, rows)], out, sem
            ).start()

        @pl.when(kind_ref[slot] == 1)
        def _():
            for way in range(WAYS):
                shift = (source_ref[slot] - way * stride + peers) % peers
                pltpu.make_async_copy(
                    staged.at[shift, pl.ds(rows, tall)], out.at[pl.ds(way * tall, tall)], sem
                ).start()

        @pl.when(kind_ref[slot] == 2)
        def _():
            copy = pltpu.make_async_copy(
                second.at[source_ref[slot]], extra.at[slot], in_sems.at[peers + slot]
            )
            copy.start()
            copy.wait()
            pltpu.make_async_copy(extra.at[slot], out, sem).start()

    for slot in range(kind_ref.shape[0]):
        out = outs[slot // room].at[slot % room]
        pltpu.make_async_copy(extra.at[slot], out, out_sems.at[slot]).wait()


def attend(q_ref, k_ref, v_ref, mixed_ref, shifted):
    tiles, count, _ = v_ref.shape
    head_of = lax.broadcasted_iota(jnp.int32, (count, LANES), 1) // HEAD_DIM
    per_tile = LANES // HEAD_DIM

    def weigh(queries, keys, values, head):
        chosen = jnp.where(head_of == head, queries, jnp.zeros_like(queries))
        scores = matmul(chosen, keys, ((1,), (1,)))
        if shifted:
            scores = scores - jnp.max(scores, axis=1, keepdims=True)
        return matmul(jnp.exp2(scores).astype(BF16), values)

    if shifted:

        @pl.loop(0, tiles)
        def _(tile):
            column = pl.ds(pl.multiple_of(tile * LANES, LANES), LANES)

            @pl.loop(0, per_tile)
            def _(head):
                sums = weigh(q_ref[:, column], k_ref[:, column], v_ref[tile], head)
                mixed = (sums[:, :LANES] / sums[:, LANES:]).astype(BF16)
                mixed_ref[:, column] = jnp.where(head_of == head, mixed, mixed_ref[:, column])

        return None

    low = jnp.full((count, LANES), 1.0, F32)
    high = jnp.full((count, LANES), 1.0, F32)
    for tile in range(tiles):
        column = pl.ds(tile * LANES, LANES)
        queries, keys, values = q_ref[:, column], k_ref[:, column], v_ref[tile]
        above = jnp.zeros((count, LANES), F32)
        below = jnp.ones((count, LANES), F32)
        for head in range(per_tile):
            sums = weigh(queries, keys, values, head)
            above = jnp.where(head_of == head, sums[:, :LANES], above)
            below = jnp.where(head_of == head, sums[:, LANES:], below)
        mixed_ref[:, column] = (above / below).astype(BF16)
        low = jnp.minimum(low, below)
        high = jnp.maximum(high, below)
    return (jnp.min(low) > 2.0**-60) & (jnp.max(high) < 2.0**100)


def layer_kernel(layer, columns, peers, order_ref, *refs):
    tables, refs = refs[:2], refs[2:]
    arrived, gain_ref = refs[:columns], refs[columns]
    hbm_weights, refs = refs[columns + 1 : columns + 5], refs[columns + 5 :]
    n_out = peers + 1 + WAYS if peers else 1
    outputs, refs = refs[:n_out], refs[n_out:]
    x_ref, y_ref, q_ref, k_ref, v_ref, mixed_ref = refs[:6]
    weights, (in_sems, out_sems, w_sems) = refs[6:10], refs[10:]
    wqkv_ref, wout_ref, wup_ref, wdown_ref = weights
    patches, per_patch, rows, width = y_ref.shape
    room = arrived[0].shape[0]
    turn = pl.program_id(0)

    def load(piece):
        return pltpu.make_async_copy(
            arrived[piece], x_ref.at[pl.ds(piece * room, room)], in_sems.at[piece]
        )

    def store(action, step):
        if peers:
            send_bricks(
                action, step, y_ref.at[step], tables, outputs[:peers], outputs[peers],
                outputs[peers + 1 :], out_sems,
            )
        else:
            spot = pl.ds(step * per_patch, per_patch)
            action(pltpu.make_async_copy(y_ref.at[step], outputs[0].at[spot], out_sems.at[0, step]))

    def fetch(which):
        return pltpu.make_async_copy(
            hbm_weights[which].at[layer], weights[which], w_sems.at[which]
        )

    def arrive(which):
        @pl.when(turn == 0)
        def _():
            fetch(which).wait()

    @pl.when(turn == 0)
    def _():
        for piece in range(columns):
            load(piece).start()
        for which in range(4):
            fetch(which).start()
        v_ref[:, :, LANES:] = jnp.ones(v_ref.shape[:2] + (LANES,), BF16)
        for piece in range(columns):
            load(piece).wait()

    first = turn * per_patch
    x = jnp.concatenate([x_ref[order_ref[first + brick]] for brick in range(per_patch)], axis=0)
    normed = normalize(x.astype(F32), gain_ref[layer, 0:1, :]).astype(BF16)
    arrive(0)
    scale = math.log2(math.e) / math.sqrt(HEAD_DIM)
    q_ref[...] = (matmul(normed, wqkv_ref[:, :width]) * scale).astype(BF16)
    k_ref[...] = matmul(normed, wqkv_ref[:, width : 2 * width]).astype(BF16)
    values = matmul(normed, wqkv_ref[:, 2 * width :]).astype(BF16)
    for tile in range(width // LANES):
        v_ref[tile, :, :LANES] = values[:, tile * LANES : (tile + 1) * LANES]

    arrive(1)
    arrive(2)
    arrive(3)

    def finish(shifted):
        safe = attend(q_ref, k_ref, v_ref, mixed_ref, shifted)
        mixed = (x.astype(F32) + matmul(mixed_ref[...], wout_ref[...])).astype(BF16)
        inner = normalize(mixed.astype(F32), gain_ref[layer, 1:2, :]).astype(BF16)
        total = mixed.astype(F32)
        for begin in range(0, wup_ref.shape[1], FF_BLOCK):
            up = matmul(inner, wup_ref[:, begin : begin + FF_BLOCK])
            half = up * 0.5
            hidden = (half + half * lax.erf(up * math.sqrt(0.5))).astype(BF16)
            total = total + matmul(hidden, wdown_ref[begin : begin + FF_BLOCK, :])
        y_ref[turn] = total.astype(BF16).reshape(per_patch, rows, width)
        return safe

    safe = finish(False)

    @pl.when(jnp.logical_not(safe))
    def _():
        finish(True)

    store(start, turn)

    @pl.when(turn == patches - 1)
    def _():
        for step in range(patches):
            store(wait, step)


def send_shapes(count, rows, width, peers, tag_rows=0):
    tall = rows // WAYS
    shapes = [jax.ShapeDtypeStruct((rows + tall, width), BF16)] * peers
    shapes += [jax.ShapeDtypeStruct((max(1, count // 2), rows, width), BF16)]
    return shapes + [jax.ShapeDtypeStruct((tall + tag_rows, width), BF16)] * WAYS


def pack(points, tag, tables):
    count, rows, width = points.shape
    peers = tables[0].shape[0]
    shapes = send_shapes(count, rows, width, peers, TAG_ROWS)
    return pl.pallas_call(
        pack_kernel,
        in_specs=[SMEM] * 2 + [VMEM] * 2,
        out_specs=[HBM] * len(shapes),
        out_shape=shapes,
        scratch_shapes=[pltpu.SemaphoreType.DMA((4, max(peers, count)))],
        compiler_params=pltpu.CompilerParams(vmem_limit_bytes=8 * 2**20),
    )(*tables, tag, points)


def relay(goals, hops, payload):
    peers, ways = len(payload), len(hops)
    tall = payload[0].shape[0] // (WAYS + 1)
    return pl.pallas_call(
        functools.partial(relay_kernel, ways, hops[0].shape[0] > tall),
        in_specs=[SMEM] + [HBM] * (ways + peers),
        out_specs=[HBM] * peers,
        out_shape=[jax.ShapeDtypeStruct(slot.shape, BF16) for slot in payload],
        input_output_aliases={1 + ways + i: i for i in range(peers)},
        scratch_shapes=[
            pltpu.VMEM((ways, tall, payload[0].shape[1]), BF16),
            pltpu.VMEM((ways, TAG_ROWS, LANES), BF16),
            pltpu.SemaphoreType.DMA((2, ways)),
            pltpu.SemaphoreType.DMA((ways,)),
        ],
        compiler_params=pltpu.CompilerParams(vmem_limit_bytes=8 * 2**20),
    )(goals, *hops, *payload)


def turn_bricks(kind, source, arrived, second, columns):
    peers, slots = len(arrived), kind.shape[0]
    brick = second.shape[1:]
    return pl.pallas_call(
        functools.partial(turn_kernel, peers),
        in_specs=[SMEM] * 2 + [HBM] * (peers + 1),
        out_specs=[HBM] * columns,
        out_shape=[jax.ShapeDtypeStruct((slots // columns,) + brick, BF16)] * columns,
        scratch_shapes=[
            pltpu.VMEM((peers,) + arrived[0].shape, BF16),
            pltpu.VMEM((slots,) + brick, BF16),
            pltpu.SemaphoreType.DMA((peers + slots,)),
            pltpu.SemaphoreType.DMA((slots,)),
        ],
        compiler_params=pltpu.CompilerParams(vmem_limit_bytes=16 * 2**20),
    )(kind, source, *arrived, second)


def encoder_layer(layer, arrived, order, tables, gains, weights, last=False):
    columns = len(arrived)
    room, rows, width = arrived[0].shape
    count = order.shape[0]
    patches = count * rows // PATCH
    per_patch = PATCH // rows
    peers = 0 if last else tables[0].shape[0]
    if last:
        shapes = [jax.ShapeDtypeStruct((count, rows, width), BF16)]
    else:
        shapes = send_shapes(count, rows, width, peers)
    tokens = patches * PATCH
    dense = sum(2 * tokens * weight.shape[1] * weight.shape[2] for weight in weights)
    heads = width // HEAD_DIM
    return pl.pallas_call(
        functools.partial(layer_kernel, layer, columns, peers),
        grid=(patches,),
        in_specs=[SMEM] * 3 + [HBM] * columns + [VMEM] + [HBM] * 4,
        out_specs=[HBM] * len(shapes),
        out_shape=shapes,
        scratch_shapes=[
            pltpu.VMEM((columns * room, rows, width), BF16),
            pltpu.VMEM((patches, per_patch, rows, width), BF16),
            pltpu.VMEM((PATCH, width), BF16),
            pltpu.VMEM((PATCH, width), BF16),
            pltpu.VMEM((width // LANES, PATCH, 2 * LANES), BF16),
            pltpu.VMEM((PATCH, width), BF16),
        ]
        + [pltpu.VMEM(weight.shape[1:], BF16) for weight in weights]
        + [
            pltpu.SemaphoreType.DMA((columns,)),
            pltpu.SemaphoreType.DMA((3, max(count, peers))),
            pltpu.SemaphoreType.DMA((4,)),
        ],
        compiler_params=pltpu.CompilerParams(vmem_limit_bytes=48 * 2**20),
        cost_estimate=pl.CostEstimate(
            flops=dense + 8 * tokens * PATCH * heads * LANES,
            bytes_accessed=4 * tokens * width + sum(2 * w.shape[1] * w.shape[2] for w in weights),
            transcendentals=tokens * PATCH * heads,
        ),
    )(order, *tables, *arrived, gains, *weights)


def ranks(targets):
    count = targets.shape[-1]
    same = targets[..., :, None] == targets[..., None, :]
    earlier = jnp.arange(count)[None, :] < jnp.arange(count)[:, None]
    return jnp.sum((same & earlier).astype(jnp.int32), axis=-1)


def lookup(keys, wanted, found):
    hit = keys[..., None, :] == wanted[..., :, None]
    return jnp.sum(jnp.where(hit, found[..., None, :], 0), axis=-1)


def shifted(arrays, axis):
    size = lax.axis_size(axis)
    step = size // len(arrays)
    return [arrays[0]] + [
        lax.ppermute(arrays[d], axis, [(i, (i + d * step) % size) for i in range(size)])
        for d in range(1, len(arrays))
    ]


def per_device(points, moved_to, gains, *weights):
    count, rows, width = points.shape
    peers, columns = lax.axis_size("gx"), lax.axis_size("gy")
    row, column = lax.axis_index("gx"), lax.axis_index("gy")
    me = row * columns + column
    devices = peers * columns
    total = devices * count
    room = max(2, -(-count // columns))
    swap = functools.partial(lax.all_to_all, split_axis=0, concat_axis=0, tiled=True)
    bricks = jnp.arange(count)
    shifts = jnp.arange(peers)
    stride = peers // WAYS

    ahead = (moved_to[:, 0] // count // columns - row) % peers
    late = ranks(ahead) > 0
    pick = lookup(jnp.where(late, -1, ahead), shifts, bricks + 1) - 1
    place = jnp.where(late, jnp.cumsum(late.astype(jnp.int32), axis=1) - 1, -1)
    spare = lookup(place, jnp.arange(max(1, count // 2)), bricks + 1) - 1
    across = (moved_to[:, 1] // count - column) % columns
    across_slot = across * room + ranks(across)
    tables = [(pick[layer], spare[layer]) for layer in range(LAYERS)]

    def plan_all(moved_to):
        everyone = swap(jnp.broadcast_to(moved_to[None], (devices,) + moved_to.shape), ("gx", "gy"))
        targets = everyone[:, :, 0] // count // columns
        behind = ranks(targets) > 0
        opening = behind & (jnp.cumsum(behind.astype(jnp.int32), axis=-1) == 1)
        relayed = jnp.sum(jnp.where(opening, targets + 1, 0), axis=-1) - 1
        flat = lambda values: values.transpose(1, 0, 2).reshape(LAYERS, total)
        first, second = flat(everyone[:, :, 0]), flat(everyone[:, :, 1])
        behind = flat(behind)
        owner = jnp.arange(total) // count

        devs = jnp.arange(devices)
        lands = (first // count)[:, None, :] == devs[:, None]
        sends = owner[None, None, :] == devs[:, None]
        counts = jnp.sum(
            (jnp.stack([lands, jnp.broadcast_to(sends, lands.shape)]) & behind[:, None, :]).astype(
                jnp.int32
            ),
            axis=-1,
        )
        extra = jnp.max(counts) > 1

        across_rank = flat(ranks(everyone[:, :, 1] // count % columns))
        mine = me * count + bricks
        slots = jnp.arange(columns * room)
        every = jnp.arange(devices)
        in_column = every % columns == column
        plans = []
        for layer in range(LAYERS):
            goal = jnp.where(relayed[:, layer] >= 0, (relayed[:, layer] - row) % peers, -1)
            behind_me = jnp.where(in_column, (row - every // columns) % peers, -1)
            goals = lookup(behind_me, jnp.arange(WAYS) * stride, goal)
            origin = lookup(first[layer], mine, (row - owner // columns) % peers)
            kind = lookup(first[layer], mine, jnp.where(behind[layer], jnp.where(extra, 2, 1), 0))
            slot_kind = lookup(across_slot[layer], slots, kind)
            slot_origin = lookup(across_slot[layer], slots, origin)
            order = lookup(
                second[layer], mine, (column - owner % columns) % columns * room + across_rank[layer]
            )
            plans.append((extra, goals, slot_kind, slot_origin, order))
        return plans

    goal = jnp.sum(jnp.where(place[0] == 0, ahead[0] + 1, 0))
    tag = jnp.broadcast_to(goal.astype(BF16), (TAG_ROWS, LANES))
    made = pack(points, tag, tables[0])
    plans = plan_all(moved_to)
    for layer in range(LAYERS):
        payload, spares, hops = made[:peers], made[peers], made[peers + 1 :]
        hops = shifted(hops, "gx")
        goals = plans[layer][1] if layer else jnp.zeros((WAYS,), jnp.int32)
        payload = list(relay(goals, hops, payload))
        arrived = shifted(payload, "gx")
        extra, _, slot_kind, slot_origin, order = plans[layer]

        def send_second(spares, layer=layer):
            target = (ahead[layer] + row) % peers
            ready = lookup(jnp.where(late[layer], target, -1), shifts, place[layer])
            landed = swap(jnp.take(spares, ready, axis=0), "gx")
            return jnp.take(landed, (row - shifts) % peers, axis=0)

        def send_nothing(spares):
            return jnp.zeros((peers, rows, width), BF16)

        spares, arrived[1] = lax.optimization_barrier((spares, arrived[1]))
        seconds = lax.cond(extra, send_second, send_nothing, spares)
        arrived = turn_bricks(slot_kind, slot_origin, arrived, seconds, columns)
        arrived = shifted(arrived, "gy")
        last = layer + 1 == LAYERS
        made = encoder_layer(
            layer, arrived, order, tables[(layer + 1) % LAYERS], gains, weights, last
        )
    return made[0]


def solution(mesh):
    placed = (P(("gx", "gy"), None, None), P(None, None, ("gx", "gy")), P(), P(), P(), P(), P())
    return jax.shard_map(
        per_device,
        mesh=mesh,
        in_specs=placed,
        out_specs=P(("gx", "gy"), None, None),
        check_vma=False,
    )
```

```python
import functools
import math

import jax
import jax.numpy as jnp
from jax import lax
from jax.experimental import pallas as pl
from jax.experimental.pallas import tpu as pltpu
from jax.sharding import PartitionSpec as P

HEAD_DIM = 16
PATCH = 512
LAYERS = 2
LANES = 128
WAYS = 4
TAG_ROWS = 16
FF_BLOCK = 512
BF16 = jnp.bfloat16
F32 = jnp.float32
HBM = pl.BlockSpec(memory_space=pl.ANY)
SMEM = pl.BlockSpec(memory_space=pltpu.SMEM)
VMEM = pl.BlockSpec(memory_space=pltpu.VMEM)


def normalize(values, gain):
    center = values - jnp.mean(values, axis=1, keepdims=True)
    spread = jnp.mean(center * center, axis=1, keepdims=True)
    return center * lax.rsqrt(spread + 1e-05) * gain


def matmul(left, right, dims=((1,), (0,))):
    return lax.dot_general(left, right, (dims, ((), ())), preferred_element_type=F32)


def start(copy):
    copy.start()


def wait(copy):
    copy.wait()


def send_bricks(action, patch, bricks, tables, payload, spare, hops, sems, tag=None):
    pick_ref, spare_ref = tables
    size, rows, width = bricks.shape
    peers = len(payload)

    def here(brick):
        return (brick >= patch * size) & (brick < (patch + 1) * size)

    for shift in range(peers):
        brick = pick_ref[shift]

        @pl.when(here(brick))
        def _():
            source = bricks.at[brick - patch * size]
            action(
                pltpu.make_async_copy(source, payload[shift].at[pl.ds(0, rows)], sems.at[0, shift])
            )

    for place in range(spare.shape[0]):
        brick = spare_ref[place]

        @pl.when(here(brick))
        def _():
            source = bricks.at[brick - patch * size]
            action(pltpu.make_async_copy(source, spare.at[place], sems.at[1, place]))

    brick = spare_ref[0]

    @pl.when(here(brick))
    def _():
        source = bricks.at[brick - patch * size]
        tall = rows // len(hops)
        for way in range(len(hops)):
            window = pl.ds(way * tall, tall)
            target = hops[way].at[pl.ds(0, tall)]
            action(pltpu.make_async_copy(source.at[window], target, sems.at[2, way]))

    if tag is not None:
        tall = hops[0].shape[0] - TAG_ROWS
        for way in range(len(hops)):
            target = hops[way].at[pl.ds(tall, TAG_ROWS), pl.ds(0, LANES)]
            action(pltpu.make_async_copy(tag, target, sems.at[3, way]))


def pack_kernel(pick_ref, spare_ref, tag, points, *refs):
    peers = pick_ref.shape[0]
    payload, spare, hops, sems = refs[:peers], refs[peers], refs[peers + 1 : -1], refs[-1]
    for action in (start, wait):
        send_bricks(action, 0, points, (pick_ref, spare_ref), payload, spare, hops, sems, tag)


def relay_kernel(ways, tagged, goal_ref, *refs):
    peers = (len(refs) - 4 - ways) // 2
    hops, payload = refs[:ways], refs[ways + peers : ways + 2 * peers]
    staged, tags, in_sems, out_sems = refs[ways + 2 * peers :]
    _, tall, _ = staged.shape
    rows = payload[0].shape[0] - tall
    for action in (start, wait):
        for way in range(ways):
            source = hops[way].at[pl.ds(0, tall)]
            action(pltpu.make_async_copy(source, staged.at[way], in_sems.at[0, way]))
            if tagged:
                source = hops[way].at[pl.ds(tall, TAG_ROWS), pl.ds(0, LANES)]
                action(pltpu.make_async_copy(source, tags.at[way], in_sems.at[1, way]))
    goals = []
    for way in range(ways):
        if tagged:
            tag = jnp.max(tags[way].astype(F32)).astype(jnp.int32)
            ahead = (tag - 1 - way * (peers // ways) + peers) % peers
            goals.append(jnp.where(tag > 0, ahead, -1))
        else:
            goals.append(goal_ref[way])
    for action in (start, wait):
        for way in range(ways):
            for shift in range(peers):

                @pl.when(goals[way] == shift)
                def _():
                    target = payload[shift].at[pl.ds(rows, tall)]
                    action(pltpu.make_async_copy(staged.at[way], target, out_sems.at[way]))


def turn_kernel(peers, kind_ref, source_ref, *refs):
    arrived, second, refs = refs[:peers], refs[peers], refs[peers + 1 :]
    outs, (staged, extra, in_sems, out_sems) = refs[:-4], refs[-4:]
    room, rows, width = outs[0].shape
    tall = rows // WAYS
    stride = peers // WAYS
    for action in (start, wait):
        for shift in range(peers):
            action(pltpu.make_async_copy(arrived[shift], staged.at[shift], in_sems.at[shift]))
    for slot in range(kind_ref.shape[0]):
        out, sem = outs[slot // room].at[slot % room], out_sems.at[slot]

        @pl.when(kind_ref[slot] == 0)
        def _():
            pltpu.make_async_copy(
                staged.at[source_ref[slot], pl.ds(0, rows)], out, sem
            ).start()

        @pl.when(kind_ref[slot] == 1)
        def _():
            for way in range(WAYS):
                shift = (source_ref[slot] - way * stride + peers) % peers
                pltpu.make_async_copy(
                    staged.at[shift, pl.ds(rows, tall)], out.at[pl.ds(way * tall, tall)], sem
                ).start()

        @pl.when(kind_ref[slot] == 2)
        def _():
            copy = pltpu.make_async_copy(
                second.at[source_ref[slot]], extra.at[slot], in_sems.at[peers + slot]
            )
            copy.start()
            copy.wait()
            pltpu.make_async_copy(extra.at[slot], out, sem).start()

    for slot in range(kind_ref.shape[0]):
        out = outs[slot // room].at[slot % room]
        pltpu.make_async_copy(extra.at[slot], out, out_sems.at[slot]).wait()


def attend(q_ref, k_ref, v_ref, mixed_ref, shifted):
    tiles, count, _ = v_ref.shape
    head_of = lax.broadcasted_iota(jnp.int32, (count, LANES), 1) // HEAD_DIM
    per_tile = LANES // HEAD_DIM

    def weigh(queries, keys, values, head):
        chosen = jnp.where(head_of == head, queries, jnp.zeros_like(queries))
        scores = matmul(chosen, keys, ((1,), (1,)))
        if shifted:
            scores = scores - jnp.max(scores, axis=1, keepdims=True)
        return matmul(jnp.exp2(scores).astype(BF16), values)

    if shifted:

        @pl.loop(0, tiles)
        def _(tile):
            column = pl.ds(pl.multiple_of(tile * LANES, LANES), LANES)

            @pl.loop(0, per_tile)
            def _(head):
                sums = weigh(q_ref[:, column], k_ref[:, column], v_ref[tile], head)
                mixed = (sums[:, :LANES] / sums[:, LANES:]).astype(BF16)
                mixed_ref[:, column] = jnp.where(head_of == head, mixed, mixed_ref[:, column])

        return None

    low = jnp.full((count, LANES), 1.0, F32)
    high = jnp.full((count, LANES), 1.0, F32)
    for tile in range(tiles):
        column = pl.ds(tile * LANES, LANES)
        queries, keys, values = q_ref[:, column], k_ref[:, column], v_ref[tile]
        above = jnp.zeros((count, LANES), F32)
        below = jnp.ones((count, LANES), F32)
        for head in range(per_tile):
            sums = weigh(queries, keys, values, head)
            above = jnp.where(head_of == head, sums[:, :LANES], above)
            below = jnp.where(head_of == head, sums[:, LANES:], below)
        mixed_ref[:, column] = (above / below).astype(BF16)
        low = jnp.minimum(low, below)
        high = jnp.maximum(high, below)
    return (jnp.min(low) > 2.0**-60) & (jnp.max(high) < 2.0**100)


def layer_kernel(layer, columns, peers, order_ref, *refs):
    tables, refs = refs[:2], refs[2:]
    arrived, gain_ref = refs[:columns], refs[columns]
    hbm_weights, refs = refs[columns + 1 : columns + 5], refs[columns + 5 :]
    n_out = peers + 1 + WAYS if peers else 1
    outputs, refs = refs[:n_out], refs[n_out:]
    x_ref, y_ref, q_ref, k_ref, v_ref, mixed_ref = refs[:6]
    weights, (in_sems, out_sems, w_sems) = refs[6:10], refs[10:]
    wqkv_ref, wout_ref, wup_ref, wdown_ref = weights
    patches, per_patch, rows, width = y_ref.shape
    room = arrived[0].shape[0]
    turn = pl.program_id(0)

    def load(piece):
        return pltpu.make_async_copy(
            arrived[piece], x_ref.at[pl.ds(piece * room, room)], in_sems.at[piece]
        )

    def store(action, step):
        if peers:
            send_bricks(
                action, step, y_ref.at[step], tables, outputs[:peers], outputs[peers],
                outputs[peers + 1 :], out_sems,
            )
        else:
            spot = pl.ds(step * per_patch, per_patch)
            action(pltpu.make_async_copy(y_ref.at[step], outputs[0].at[spot], out_sems.at[0, step]))

    def fetch(which):
        return pltpu.make_async_copy(
            hbm_weights[which].at[layer], weights[which], w_sems.at[which]
        )

    def arrive(which):
        @pl.when(turn == 0)
        def _():
            fetch(which).wait()

    @pl.when(turn == 0)
    def _():
        for piece in range(columns):
            load(piece).start()
        for which in range(4):
            fetch(which).start()
        v_ref[:, :, LANES:] = jnp.ones(v_ref.shape[:2] + (LANES,), BF16)
        for piece in range(columns):
            load(piece).wait()

    first = turn * per_patch
    x = jnp.concatenate([x_ref[order_ref[first + brick]] for brick in range(per_patch)], axis=0)
    normed = normalize(x.astype(F32), gain_ref[layer, 0:1, :]).astype(BF16)
    arrive(0)
    scale = math.log2(math.e) / math.sqrt(HEAD_DIM)
    q_ref[...] = (matmul(normed, wqkv_ref[:, :width]) * scale).astype(BF16)
    k_ref[...] = matmul(normed, wqkv_ref[:, width : 2 * width]).astype(BF16)
    values = matmul(normed, wqkv_ref[:, 2 * width :]).astype(BF16)
    for tile in range(width // LANES):
        v_ref[tile, :, :LANES] = values[:, tile * LANES : (tile + 1) * LANES]

    def finish(shifted):
        safe = attend(q_ref, k_ref, v_ref, mixed_ref, shifted)
        if not shifted:
            arrive(1)
            arrive(2)
            arrive(3)
        mixed = (x.astype(F32) + matmul(mixed_ref[...], wout_ref[...])).astype(BF16)
        inner = normalize(mixed.astype(F32), gain_ref[layer, 1:2, :]).astype(BF16)
        total = mixed.astype(F32)
        for begin in range(0, wup_ref.shape[1], FF_BLOCK):
            up = matmul(inner, wup_ref[:, begin : begin + FF_BLOCK])
            half = up * 0.5
            hidden = (half + half * lax.erf(up * math.sqrt(0.5))).astype(BF16)
            total = total + matmul(hidden, wdown_ref[begin : begin + FF_BLOCK, :])
        y_ref[turn] = total.astype(BF16).reshape(per_patch, rows, width)
        return safe

    safe = finish(False)

    @pl.when(jnp.logical_not(safe))
    def _():
        finish(True)

    store(start, turn)

    @pl.when(turn == patches - 1)
    def _():
        for step in range(patches):
            store(wait, step)


def send_shapes(count, rows, width, peers, tag_rows=0):
    tall = rows // WAYS
    shapes = [jax.ShapeDtypeStruct((rows + tall, width), BF16)] * peers
    shapes += [jax.ShapeDtypeStruct((max(1, count // 2), rows, width), BF16)]
    return shapes + [jax.ShapeDtypeStruct((tall + tag_rows, width), BF16)] * WAYS


def pack(points, tag, tables):
    count, rows, width = points.shape
    peers = tables[0].shape[0]
    shapes = send_shapes(count, rows, width, peers, TAG_ROWS)
    return pl.pallas_call(
        pack_kernel,
        in_specs=[SMEM] * 2 + [VMEM] * 2,
        out_specs=[HBM] * len(shapes),
        out_shape=shapes,
        scratch_shapes=[pltpu.SemaphoreType.DMA((4, max(peers, count)))],
        compiler_params=pltpu.CompilerParams(vmem_limit_bytes=8 * 2**20),
    )(*tables, tag, points)


def relay(goals, hops, payload):
    peers, ways = len(payload), len(hops)
    tall = payload[0].shape[0] // (WAYS + 1)
    return pl.pallas_call(
        functools.partial(relay_kernel, ways, hops[0].shape[0] > tall),
        in_specs=[SMEM] + [HBM] * (ways + peers),
        out_specs=[HBM] * peers,
        out_shape=[jax.ShapeDtypeStruct(slot.shape, BF16) for slot in payload],
        input_output_aliases={1 + ways + i: i for i in range(peers)},
        scratch_shapes=[
            pltpu.VMEM((ways, tall, payload[0].shape[1]), BF16),
            pltpu.VMEM((ways, TAG_ROWS, LANES), BF16),
            pltpu.SemaphoreType.DMA((2, ways)),
            pltpu.SemaphoreType.DMA((ways,)),
        ],
        compiler_params=pltpu.CompilerParams(vmem_limit_bytes=8 * 2**20),
    )(goals, *hops, *payload)


def turn_bricks(kind, source, arrived, second, columns):
    peers, slots = len(arrived), kind.shape[0]
    brick = second.shape[1:]
    return pl.pallas_call(
        functools.partial(turn_kernel, peers),
        in_specs=[SMEM] * 2 + [HBM] * (peers + 1),
        out_specs=[HBM] * columns,
        out_shape=[jax.ShapeDtypeStruct((slots // columns,) + brick, BF16)] * columns,
        scratch_shapes=[
            pltpu.VMEM((peers,) + arrived[0].shape, BF16),
            pltpu.VMEM((slots,) + brick, BF16),
            pltpu.SemaphoreType.DMA((peers + slots,)),
            pltpu.SemaphoreType.DMA((slots,)),
        ],
        compiler_params=pltpu.CompilerParams(vmem_limit_bytes=16 * 2**20),
    )(kind, source, *arrived, second)


def encoder_layer(layer, arrived, order, tables, gains, weights, last=False):
    columns = len(arrived)
    room, rows, width = arrived[0].shape
    count = order.shape[0]
    patches = count * rows // PATCH
    per_patch = PATCH // rows
    peers = 0 if last else tables[0].shape[0]
    if last:
        shapes = [jax.ShapeDtypeStruct((count, rows, width), BF16)]
    else:
        shapes = send_shapes(count, rows, width, peers)
    tokens = patches * PATCH
    dense = sum(2 * tokens * weight.shape[1] * weight.shape[2] for weight in weights)
    heads = width // HEAD_DIM
    return pl.pallas_call(
        functools.partial(layer_kernel, layer, columns, peers),
        grid=(patches,),
        in_specs=[SMEM] * 3 + [HBM] * columns + [VMEM] + [HBM] * 4,
        out_specs=[HBM] * len(shapes),
        out_shape=shapes,
        scratch_shapes=[
            pltpu.VMEM((columns * room, rows, width), BF16),
            pltpu.VMEM((patches, per_patch, rows, width), BF16),
            pltpu.VMEM((PATCH, width), BF16),
            pltpu.VMEM((PATCH, width), BF16),
            pltpu.VMEM((width // LANES, PATCH, 2 * LANES), BF16),
            pltpu.VMEM((PATCH, width), BF16),
        ]
        + [pltpu.VMEM(weight.shape[1:], BF16) for weight in weights]
        + [
            pltpu.SemaphoreType.DMA((columns,)),
            pltpu.SemaphoreType.DMA((3, max(count, peers))),
            pltpu.SemaphoreType.DMA((4,)),
        ],
        compiler_params=pltpu.CompilerParams(vmem_limit_bytes=48 * 2**20),
        cost_estimate=pl.CostEstimate(
            flops=dense + 8 * tokens * PATCH * heads * LANES,
            bytes_accessed=4 * tokens * width + sum(2 * w.shape[1] * w.shape[2] for w in weights),
            transcendentals=tokens * PATCH * heads,
        ),
    )(order, *tables, *arrived, gains, *weights)


def ranks(targets):
    count = targets.shape[-1]
    same = targets[..., :, None] == targets[..., None, :]
    earlier = jnp.arange(count)[None, :] < jnp.arange(count)[:, None]
    return jnp.sum((same & earlier).astype(jnp.int32), axis=-1)


def lookup(keys, wanted, found):
    hit = keys[..., None, :] == wanted[..., :, None]
    return jnp.sum(jnp.where(hit, found[..., None, :], 0), axis=-1)


def shifted(arrays, axis):
    size = lax.axis_size(axis)
    step = size // len(arrays)
    return [arrays[0]] + [
        lax.ppermute(arrays[d], axis, [(i, (i + d * step) % size) for i in range(size)])
        for d in range(1, len(arrays))
    ]


def per_device(points, moved_to, gains, *weights):
    count, rows, width = points.shape
    peers, columns = lax.axis_size("gx"), lax.axis_size("gy")
    row, column = lax.axis_index("gx"), lax.axis_index("gy")
    me = row * columns + column
    devices = peers * columns
    total = devices * count
    room = max(2, -(-count // columns))
    swap = functools.partial(lax.all_to_all, split_axis=0, concat_axis=0, tiled=True)
    bricks = jnp.arange(count)
    shifts = jnp.arange(peers)
    stride = peers // WAYS

    ahead = (moved_to[:, 0] // count // columns - row) % peers
    late = ranks(ahead) > 0
    pick = lookup(jnp.where(late, -1, ahead), shifts, bricks + 1) - 1
    place = jnp.where(late, jnp.cumsum(late.astype(jnp.int32), axis=1) - 1, -1)
    spare = lookup(place, jnp.arange(max(1, count // 2)), bricks + 1) - 1
    across = (moved_to[:, 1] // count - column) % columns
    across_slot = across * room + ranks(across)
    tables = [(pick[layer], spare[layer]) for layer in range(LAYERS)]

    def plan_all(moved_to):
        everyone = swap(jnp.broadcast_to(moved_to[None], (devices,) + moved_to.shape), ("gx", "gy"))
        targets = everyone[:, :, 0] // count // columns
        behind = ranks(targets) > 0
        opening = behind & (jnp.cumsum(behind.astype(jnp.int32), axis=-1) == 1)
        relayed = jnp.sum(jnp.where(opening, targets + 1, 0), axis=-1) - 1
        flat = lambda values: values.transpose(1, 0, 2).reshape(LAYERS, total)
        first, second = flat(everyone[:, :, 0]), flat(everyone[:, :, 1])
        behind = flat(behind)
        owner = jnp.arange(total) // count

        devs = jnp.arange(devices)
        lands = (first // count)[:, None, :] == devs[:, None]
        sends = owner[None, None, :] == devs[:, None]
        counts = jnp.sum(
            (jnp.stack([lands, jnp.broadcast_to(sends, lands.shape)]) & behind[:, None, :]).astype(
                jnp.int32
            ),
            axis=-1,
        )
        extra = jnp.max(counts) > 1

        across_rank = flat(ranks(everyone[:, :, 1] // count % columns))
        mine = me * count + bricks
        slots = jnp.arange(columns * room)
        every = jnp.arange(devices)
        in_column = every % columns == column
        plans = []
        for layer in range(LAYERS):
            goal = jnp.where(relayed[:, layer] >= 0, (relayed[:, layer] - row) % peers, -1)
            behind_me = jnp.where(in_column, (row - every // columns) % peers, -1)
            goals = lookup(behind_me, jnp.arange(WAYS) * stride, goal)
            origin = lookup(first[layer], mine, (row - owner // columns) % peers)
            kind = lookup(first[layer], mine, jnp.where(behind[layer], jnp.where(extra, 2, 1), 0))
            slot_kind = lookup(across_slot[layer], slots, kind)
            slot_origin = lookup(across_slot[layer], slots, origin)
            order = lookup(
                second[layer], mine, (column - owner % columns) % columns * room + across_rank[layer]
            )
            plans.append((extra, goals, slot_kind, slot_origin, order))
        return plans

    goal = jnp.sum(jnp.where(place[0] == 0, ahead[0] + 1, 0))
    tag = jnp.broadcast_to(goal.astype(BF16), (TAG_ROWS, LANES))
    made = pack(points, tag, tables[0])
    plans = plan_all(moved_to)
    for layer in range(LAYERS):
        payload, spares, hops = made[:peers], made[peers], made[peers + 1 :]
        hops = shifted(hops, "gx")
        goals = plans[layer][1] if layer else jnp.zeros((WAYS,), jnp.int32)
        payload = list(relay(goals, hops, payload))
        arrived = shifted(payload, "gx")
        extra, _, slot_kind, slot_origin, order = plans[layer]

        def send_second(spares, layer=layer):
            target = (ahead[layer] + row) % peers
            ready = lookup(jnp.where(late[layer], target, -1), shifts, place[layer])
            landed = swap(jnp.take(spares, ready, axis=0), "gx")
            return jnp.take(landed, (row - shifts) % peers, axis=0)

        def send_nothing(spares):
            return jnp.zeros((peers, rows, width), BF16)

        spares, arrived[1] = lax.optimization_barrier((spares, arrived[1]))
        seconds = lax.cond(extra, send_second, send_nothing, spares)
        arrived = turn_bricks(slot_kind, slot_origin, arrived, seconds, columns)
        arrived = shifted(arrived, "gy")
        last = layer + 1 == LAYERS
        made = encoder_layer(
            layer, arrived, order, tables[(layer + 1) % LAYERS], gains, weights, last
        )
    return made[0]


def solution(mesh):
    placed = (P(("gx", "gy"), None, None), P(None, None, ("gx", "gy")), P(), P(), P(), P(), P())
    return jax.shard_map(
        per_device,
        mesh=mesh,
        in_specs=placed,
        out_specs=P(("gx", "gy"), None, None),
        check_vma=False,
    )
```
